128 devices in a mesh: fsdp: 16 (over z_lo, x, core), dp: 8 (over z_hi, y).
Axes of the slice: x: 4, y: 4, z: 4 (z_hi: 2, z_lo: 2; z = z_hi * 2 + z_lo), core: 2. Of those that a mesh axis runs over, the one named last changes fastest.
Arguments:
- tokens: bfloat16 [16384, 2048], P(('fsdp', 'dp')), may hold values from -6 to 6
- segment_ids: int32 [256, 64], P(('fsdp', 'dp')), may hold values from 0 to 1, never falling along the last dimension, each value on 1 to 48 neighbouring positions
- ln1_gain: bfloat16 [2048], P(('fsdp', 'dp')), may hold values from 0.5 to 1.5
- ln1_bias: bfloat16 [2048], P(('fsdp', 'dp')), may hold values from -1.75 to 1.75
- w_qkv: bfloat16 [2048, 6144], P(('fsdp', 'dp')), may hold values from -0.125 to 0.125
- qkv_bias: bfloat16 [3, 2048], P(None, ('fsdp', 'dp')), may hold values from -3 to 3
- w_out: bfloat16 [2048, 2048], P(('fsdp', 'dp')), may hold values from -0.375 to 0.375
- ln2_gain: bfloat16 [2048], P(('fsdp', 'dp')), may hold values from 0.5 to 1.5
- ln2_bias: bfloat16 [2048], P(('fsdp', 'dp')), may hold values from -1.75 to 1.75
- w_gate: bfloat16 [2048, 5632], P(('fsdp', 'dp')), may hold values from -0.125 to 0.125
- w_up: bfloat16 [2048, 5632], P(('fsdp', 'dp')), may hold values from -0.125 to 0.125
- w_down: bfloat16 [5632, 2048], P(('fsdp', 'dp')), may hold values from -0.078125 to 0.078125
- cotangent: bfloat16 [16384, 2048], P(('fsdp', 'dp')), may hold values from -6 to 6
Outputs:
- out: bfloat16 [16384, 2048], P(('fsdp', 'dp'))
- grad_tokens: float32 [16384, 2048], P(('fsdp', 'dp'))
- grad_ln1_gain: float32 [2048], P(('fsdp', 'dp'))
- grad_ln1_bias: float32 [2048], P(('fsdp', 'dp'))
- grad_w_qkv: float32 [2048, 6144], P(('fsdp', 'dp'))
- grad_qkv_bias: float32 [3, 2048], P(None, ('fsdp', 'dp'))
- grad_w_out: float32 [2048, 2048], P(('fsdp', 'dp'))
- grad_ln2_gain: float32 [2048], P(('fsdp', 'dp'))
- grad_ln2_bias: float32 [2048], P(('fsdp', 'dp'))
- grad_w_gate: float32 [2048, 5632], P(('fsdp', 'dp'))
- grad_w_up: float32 [2048, 5632], P(('fsdp', 'dp'))
- grad_w_down: float32 [5632, 2048], P(('fsdp', 'dp'))
The draws below stay inside these ranges and needn't reach their ends.
Inputs may be any that keep to these rules, and one draw needn't show every extreme that they name: `segment_ids`: in every row (one micro-batch of 64 slots) the segment numbers never fall, each of the 2 sequences holds 1 to 48 slots.
All inputs are finite; a program needn't handle non-finite values.
Results may differ from the reference program's by a relative error of at most 0.014.
Values may be sent and summed in bfloat16 or wider, within the bound.
A program may use at most 576 MiB of HBM per device.

```python
import math
import jax
import jax.numpy as jnp
import numpy as np
from jax import lax

D = 2048
HEADS = 32
ROT = 16
FF = 5632
SLOT = 64
SEGS = 2
LONGEST = 48
BLOCKS = 256
TOKENS = 16384


def levels(own_key, dims, shards, least, high):
    loudness, own = 1.0, jax.random.fold_in(own_key, 6)
    for dim, parts in shards:
        draws = jnp.exp(jax.random.uniform(jax.random.fold_in(own, dim), (parts,), jnp.float32, least / len(shards), high / len(shards)))
        loudness = loudness * jnp.repeat(draws, dims[dim] // parts).reshape([-1 if axis == dim else 1 for axis in range(len(dims))])
    return loudness


def split_up(number_of, total, reach, lean):
    loads = [(1 << 20) // math.isqrt(standing ** lean) + 1 for standing in range(2, number_of + 1)]
    rest, counts = total - reach - (number_of - 1), [1] * (number_of - 1)
    while rest > 0:
        movable = [i for i in range(number_of - 1) if counts[i] < reach]
        whole, remaining = sum([loads[i] for i in movable]), rest
        for i in movable:
            addition = min(reach - counts[i], max(1, remaining * loads[i] // whole), rest)
            counts[i] = counts[i] + addition
            rest = rest - addition
    return np.array([reach] + counts)


def uneven_parts(rng, number_of, total, most, slope):
    if number_of == 2:
        one = jax.random.randint(rng, (), max(1, total - most), min(most, total - 1) + 1)
        return jnp.stack([one, total - one])
    sizes = jnp.asarray(split_up(number_of, total, most, slope), jnp.int32)
    pairs = (number_of - 1) // 2
    donor, receiver = sizes[1:1 + 2 * pairs:2], sizes[2:2 + 2 * pairs:2]
    slack = jnp.minimum(donor - 1, most - receiver)
    passed = jax.random.randint(jax.random.fold_in(rng, 1), (pairs,), 0, 1 << 20) % (slack + 1)
    sizes = sizes.at[1:1 + 2 * pairs:2].set(donor - passed).at[2:2 + 2 * pairs:2].set(receiver + passed)
    return sizes[jax.random.permutation(jax.random.fold_in(rng, 2), number_of)]


def gaussian(rng, dims, deviation, bound, shards=(), kind=jnp.bfloat16):
    values = jax.random.normal(rng, dims, jnp.float32) * deviation
    if len(shards) > 0:
        values = levels(rng, dims, shards, -0.22, 0.18) * values
    return jnp.clip(values, min=-bound, max=bound).astype(kind)


def setup_inputs(seed: int = 0) -> dict:
    key_of = jax.random.split(jax.random.key(seed), 14)
    tokens = gaussian(key_of[0], (TOKENS, D), 1.0, 6.0, ((0, 128),))
    segment_ids = jax.vmap(lambda own: jnp.searchsorted(jnp.cumsum(uneven_parts(own, SEGS, SLOT, LONGEST, 0)), jnp.arange(SLOT), side="right"))(jax.random.split(key_of[1], BLOCKS)).reshape((BLOCKS, SLOT)).astype(jnp.int32)
    ln1_gain = jnp.clip(1.0 + 0.1 * jax.random.normal(key_of[2], (D,), jnp.float32), 0.5, 1.5).astype(jnp.bfloat16)
    ln1_bias = gaussian(key_of[3], (D,), 0.3, 1.75, ((0, 128),))
    w_qkv = gaussian(key_of[4], (D, 3 * D), D ** -0.5, 0.125, ((0, 128),))
    qkv_bias = gaussian(key_of[5], (3, D), 0.5, 3.0, ((1, 128),))
    w_out = gaussian(key_of[6], (D, D), (D // 8) ** -0.5, 0.375, ((0, 128),))
    ln2_gain = jnp.clip(1.0 + 0.1 * jax.random.normal(key_of[7], (D,), jnp.float32), 0.5, 1.5).astype(jnp.bfloat16)
    ln2_bias = gaussian(key_of[8], (D,), 0.3, 1.75, ((0, 128),))
    w_gate = gaussian(key_of[9], (D, FF), D ** -0.5, 0.125, ((0, 128),))
    w_up = gaussian(key_of[10], (D, FF), D ** -0.5, 0.125, ((0, 128),))
    w_down = gaussian(key_of[11], (FF, D), FF ** -0.5, 0.078125, ((0, 128),))
    cotangent = gaussian(key_of[12], (TOKENS, D), 1.0, 6.0, ((0, 128),))
    return {"tokens": tokens, "segment_ids": segment_ids, "ln1_gain": ln1_gain, "ln1_bias": ln1_bias, "w_qkv": w_qkv, "qkv_bias": qkv_bias, "w_out": w_out, "ln2_gain": ln2_gain, "ln2_bias": ln2_bias, "w_gate": w_gate, "w_up": w_up, "w_down": w_down, "cotangent": cotangent}


EPS = 1e-05
THETA = 10000.0
precise = lax.Precision.HIGHEST

@jax.custom_vjp
def low(v):
    return lax.optimization_barrier(v.astype(jnp.bfloat16)).astype(jnp.float32)

@jax.custom_vjp
def low_back(v):
    return v

def low_keep(v):
    return (low(v), None)

def low_pass(kept, grad):
    return (grad,)

def back_keep(v):
    return (v, None)

def back_low(kept, grad):
    return (low(grad),)
low.defvjp(low_keep, low_pass)
low_back.defvjp(back_keep, back_low)

def layer_norm(values, gain_vec, bias_vec):
    average = lax.optimization_barrier(jnp.mean(values, axis=1, keepdims=True))
    centred = values - average
    spread = lax.optimization_barrier(jnp.mean(centred * centred, axis=1, keepdims=True))
    return centred * lax.rsqrt(spread + EPS) * gain_vec + bias_vec

def rotary_tables(segments):
    slot_len = segments.shape[1]
    earlier = (segments[:, None, :] < segments[:, :, None]).astype(jnp.int32)
    position = jnp.arange(slot_len, dtype=jnp.int32)[None, :] - lax.optimization_barrier(jnp.sum(earlier, axis=2, dtype=jnp.int32))
    half_dims = ROT // 2
    inverse = THETA ** (-2.0 * jnp.arange(half_dims, dtype=jnp.float32) / ROT)
    angles = position.reshape(-1, 1).astype(jnp.float32) * inverse[None, :]
    angles = jnp.concatenate([angles, angles], axis=1)
    return (jnp.cos(angles), jnp.sin(angles))

def rotate(values, cosine_table, sine_table):
    token_count, model_width = values.shape
    by_head = values.reshape(token_count, HEADS, model_width // HEADS)
    half_dims = ROT // 2
    turned = by_head[:, :, :ROT]
    swapped = jnp.concatenate([-turned[:, :, half_dims:], turned[:, :, :half_dims]], axis=2)
    turned = turned * cosine_table[:, None, :] + swapped * sine_table[:, None, :]
    return jnp.concatenate([turned, by_head[:, :, ROT:]], axis=2).reshape(token_count, model_width)

def forward(inputs, params, segments):
    ln1_gain, ln1_bias, w_qkv, qkv_bias, w_out, ln2_gain, ln2_bias, w_gate, w_up, w_down = params
    token_count, model_width = inputs.shape
    group_count, slot_len = segments.shape
    head_dim = model_width // HEADS
    xn_one = low(layer_norm(inputs, ln1_gain, ln1_bias))
    projected = low_back(jnp.dot(xn_one, w_qkv, precision=precise) + qkv_bias.reshape(-1))
    cosine_table, sine_table = rotary_tables(segments)
    queries = low(rotate(projected[:, :model_width], cosine_table, sine_table))
    keys = low(rotate(projected[:, model_width:2 * model_width], cosine_table, sine_table))
    values = low(projected[:, 2 * model_width:])
    block_shape = (group_count, slot_len, HEADS, head_dim)
    scores = jnp.einsum('bqhd,bkhd->bhqk', queries.reshape(block_shape), keys.reshape(block_shape), precision=precise)
    scores = low_back(scores * head_dim ** (-0.5))
    same_segment = segments[:, :, None] == segments[:, None, :]
    causal = jnp.arange(slot_len)[None, :] <= jnp.arange(slot_len)[:, None]
    allowed = (same_segment & causal[None, :, :])[:, None, :, :]
    scores = jnp.where(allowed, scores, -1e+30)
    largest = lax.optimization_barrier(jnp.max(scores, axis=3, keepdims=True))
    shifted = jnp.exp(scores - largest)
    attn_probs = shifted / lax.optimization_barrier(jnp.sum(shifted, axis=3, keepdims=True))
    mixed_sum = jnp.einsum('bhqk,bkhd->bqhd', low(attn_probs), values.reshape(block_shape), precision=precise)
    mixed_low = low(low_back(mixed_sum.reshape(token_count, model_width)))
    residual = inputs + low_back(jnp.dot(mixed_low, w_out, precision=precise))
    xn_two = low(layer_norm(residual, ln2_gain, ln2_bias))
    gate_val = low_back(jnp.dot(xn_two, w_gate, precision=precise))
    up_val = low_back(jnp.dot(xn_two, w_up, precision=precise))
    hidden = low(gate_val * jax.nn.sigmoid(gate_val) * up_val)
    return residual + low_back(jnp.dot(hidden, w_down, precision=precise))

def reference(tokens, segment_ids, ln1_gain, ln1_bias, w_qkv, qkv_bias, w_out, ln2_gain, ln2_bias, w_gate, w_up, w_down, cotangent):
    params = tuple((weight_arr.astype(jnp.float32) for weight_arr in (ln1_gain, ln1_bias, w_qkv, qkv_bias, w_out, ln2_gain, ln2_bias, w_gate, w_up, w_down)))
    group_blocks = math.gcd(BLOCKS, max(1, 4096 // SLOT))
    group_count = BLOCKS // group_blocks
    group_rows = group_blocks * SLOT
    inputs = tokens.astype(jnp.float32).reshape(group_count, group_rows, D)
    grads_in = cotangent.astype(jnp.float32).reshape(group_count, group_rows, D)
    segments = segment_ids.reshape(group_count, group_blocks, SLOT)

    def step(running, pieces):
        x_part, seg_part, ct_part = pieces

        def layer_fn(x_value, param_values):
            return forward(x_value, param_values, seg_part)
        result, pullback = jax.vjp(layer_fn, x_part, params)
        grad_x, grad_params = pullback(ct_part)
        running = tuple((total + grad for total, grad in zip(running, grad_params)))
        return (running, (result, grad_x))
    zeros = tuple((jnp.zeros_like(weight_arr) for weight_arr in params))
    totals, outputs = lax.scan(step, zeros, (inputs, segments, grads_in))
    results, grad_x = outputs
    return (results.reshape(TOKENS, D).astype(jnp.bfloat16), grad_x.reshape(TOKENS, D), totals[0], totals[1], totals[2], totals[3], totals[4], totals[5], totals[6], totals[7], totals[8], totals[9])
```

```python
import jax
import jax.numpy as jnp
import numpy as np
from jax import lax
from jax.experimental import pallas as pl
from jax.experimental.pallas import tpu as pltpu
from jax.sharding import PartitionSpec as P

HEADS = 32
ROT = 16
LONGEST = 48
EPS = 1e-05
THETA = 10000.0
MESH = pl.DeviceIdType.MESH
BF = jnp.bfloat16
F32 = jnp.float32


def rem(a, n):
    return a % n if isinstance(a, int) else lax.rem(a, n)


def div(a, n):
    return a // n if isinstance(a, int) else lax.div(a, n)


class Net:
    def __init__(self, send_sems, recv_sems, local_sems):
        f, d = lax.axis_index("fsdp"), lax.axis_index("dp")
        self.zl, self.x, self.c = div(f, 8), rem(div(f, 2), 4), rem(f, 2)
        self.zh, self.y = div(d, 4), rem(d, 4)
        self.z = self.zh * 2 + self.zl
        self.xc = rem(f, 8)
        self.send_sems, self.recv_sems, self.local_sems = send_sems, recv_sems, local_sems
        self.count, self.locals = 0, 0
        self.sent, self.stream = [], ""

    def at(self, x=0, y=0, z=0, c=0):
        xx, yy = rem(self.x + x + 4, 4), rem(self.y + y + 4, 4)
        zz, cc = rem(self.z + z + 4, 4), rem(self.c + c, 2)
        return {"fsdp": rem(zz, 2) * 8 + xx * 2 + cc, "dp": div(zz, 2) * 4 + yy}

    def peer(self, xc):
        return {"fsdp": self.zl * 8 + xc, "dp": self.zh * 4 + self.y}

    def send(self, src, dst, device):
        copy = pltpu.make_async_remote_copy(
            src_ref=src, dst_ref=dst, send_sem=self.send_sems.at[self.count],
            recv_sem=self.recv_sems.at[self.count], device_id=device, device_id_type=MESH)
        self.count += 1
        copy.start()
        self.sent.append((self.stream, copy))
        return copy

    def local(self, src, dst):
        copy = pltpu.make_async_copy(src, dst, self.local_sems.at[self.locals])
        self.locals += 1
        copy.start()
        return copy

    def work(self, cost, fn):
        fn()

    def drain(self, streams):
        for stream, copy in self.sent:
            if stream in streams:
                copy.wait_send()
        self.sent = [entry for entry in self.sent if entry[0] not in streams]

    def finish(self):
        for _, copy in self.sent:
            copy.wait_send()


def greet(net, groups, far=False):
    devices = [net.at(y=1), net.at(y=-1), net.at(z=1), net.at(z=-1)]
    if groups:
        devices += [net.peer(rem(net.xc + k, 8)) for k in range(1, 8)]
    else:
        devices += [net.at(x=1), net.at(x=-1), net.at(c=1)]
    if far:
        devices += [net.at(y=2), net.at(z=2)]
    barrier = pltpu.get_barrier_semaphore()
    for device in devices:
        pl.semaphore_signal(barrier, inc=1, device_id=device, device_id_type=MESH)
    pl.semaphore_wait(barrier, len(devices))


def play(net, order, **streams):
    marks = set()

    def step(letter):
        before, net.stream = net.stream, letter
        try:
            next(streams[letter])
        except StopIteration:
            del streams[letter]
        net.stream = before

    def need(letters, mark=None):
        for letter in letters:
            while letter in streams and (letter, mark) not in marks:
                step(letter)
    net.need = need
    net.mark = lambda mark: marks.add((net.stream, mark))
    for letter in "".join(order):
        if letter in streams:
            step(letter)
    while streams:
        for letter in list(streams):
            if letter in streams:
                step(letter)


def gather_xc(net, *pairs):
    x, c = net.x, net.c
    right, left, sib = net.at(x=1), net.at(x=-1), net.at(c=1)
    xm, xp, xo = rem(x + 3, 4), rem(x + 1, 4), rem(x + 2, 4)

    def send(whole, device):
        return [net.send(src, dst, device) for src, dst in whole]

    def wait(copies):
        for copy in copies:
            copy.wait_recv()

    def part(k, rows=None):
        refs = [dst.at[k, c] if rows is None else dst.at[k, c, rows(dst.shape[2])] for _, dst in pairs]
        return [(ref, ref) for ref in refs]
    own = [(src, dst.at[x, c]) for src, dst in pairs]
    here = [net.local(src, dst) for src, dst in own]
    r, l, s0 = send(own, right), send(own, left), send(own, sib)
    yield
    wait(r)
    r2 = send(part(xm, lambda n: pl.ds(0, n // 2)), right)
    s1 = send(part(xm), sib)
    wait(l)
    l2 = send(part(xp, lambda n: pl.ds(n // 2, n // 2)), left)
    s2 = send(part(xp), sib)
    yield
    wait(r2)
    wait(l2)
    s3 = send(part(xo), sib)
    yield
    for copy in here:
        copy.wait()
    for copies in (s0, s1, s2, s3):
        wait(copies)


def gather_ring(net, view, p, plus, minus):
    own = view(p, None)
    a = net.send(own, own, plus)
    b = net.send(own, own, minus)
    yield
    pm, pp = rem(p + 3, 4), rem(p + 1, 4)
    a.wait_recv()
    a2 = net.send(view(pm, 0), view(pm, 0), plus)
    b.wait_recv()
    b2 = net.send(view(pp, 1), view(pp, 1), minus)
    yield
    a2.wait_recv()
    b2.wait_recv()


def columns_view(ref):
    def view(z, y, quarter, quarters):
        q = pl.ds(2 * quarter, 2 * quarters)
        if y is None:
            return ref.at[rem(z, 2), q, div(z, 2)]
        if z is None:
            return ref.at[:, q, :, y]
        return ref.at[rem(z, 2), q, div(z, 2), y]
    return view


def rows_view(ref):
    width = ref.shape[-1] // 4

    def view(z, y, quarter, quarters):
        q = pl.ds(width * quarter, width * quarters)
        if y is None:
            return ref.at[rem(z, 2), div(z, 2), :, :, q]
        if z is None:
            return ref.at[:, :, y, :, q]
        return ref.at[rem(z, 2), div(z, 2), y, :, q]
    return view


def gather_yz(net, view, first):
    def pick(base, place):
        def at(p, half):
            quarter, quarters = (base, 2) if half is None else (base + half, 1)
            return place(p, quarter, quarters)
        return at
    up_y, down_y, up_z, down_z = net.at(y=1), net.at(y=-1), net.at(z=1), net.at(z=-1)
    if first == "y":
        yield from gather_ring(net, pick(0, lambda p, q, n: view(net.z, p, q, n)), net.y, up_y, down_y)
        yield from gather_ring(net, pick(0, lambda p, q, n: view(p, None, q, n)), net.z, up_z, down_z)
    else:
        yield from gather_ring(net, pick(2, lambda p, q, n: view(p, net.y, q, n)), net.z, up_z, down_z)
        yield from gather_ring(net, pick(2, lambda p, q, n: view(None, p, q, n)), net.y, up_y, down_y)


def sum_xc(net, theirs, own, r1, ra, rb, r2p, r2m):
    half = ra.shape[1]
    x = net.x
    right, left, sib = net.at(x=1), net.at(x=-1), net.at(c=1)
    xm, xp, xo = rem(x + 3, 4), rem(x + 1, 4), rem(x + 2, 4)
    first, second = pl.ds(0, half), pl.ds(half, half)
    s = [net.send(theirs(k), r1.at[k], sib) for k in (xo, xm, xp, x)]
    yield
    def add(k):
        def go():
            r1[k] = r1[k] + own(k)[...]
        net.work(0.2, go)
    s[0].wait_recv()
    add(xo)
    a = net.send(r1.at[xo, :, first], ra, left)
    b = net.send(r1.at[xo, :, second], rb, right)
    s[1].wait_recv()
    add(xm)
    c1 = net.send(r1.at[xm, :, second], r2p.at[:, second], left)
    s[2].wait_recv()
    add(xp)
    c2 = net.send(r1.at[xp, :, first], r2m.at[:, first], right)
    yield
    a.wait_recv()

    def add_a():
        ra[...] = ra[...] + r1[xm, :, first]

    def add_b():
        rb[...] = rb[...] + r1[xp, :, second]
    net.work(0.1, add_a)
    d1 = net.send(ra, r2p.at[:, first], left)
    b.wait_recv()
    net.work(0.1, add_b)
    d2 = net.send(rb, r2m.at[:, second], right)
    yield
    s[3].wait_recv()
    for copy in (c1, c2, d1, d2):
        copy.wait_recv()


def sum_xc_scratch(rows, n):
    return [pltpu.VMEM((4, rows, n), BF), pltpu.VMEM((rows, n // 2), BF), pltpu.VMEM((rows, n // 2), BF),
            pltpu.VMEM((rows, n), BF), pltpu.VMEM((rows, n), BF)]


def four_terms(net, own, scratch, rows):
    r1, _, _, r2p, r2m = scratch
    return (own(net.x)[rows].astype(F32) + r1[net.x, rows].astype(F32)
            + r2p[rows].astype(F32) + r2m[rows].astype(F32))


def sum_ring(net, view, p, plus, minus, ra, rb, rp, rm, put, source=None):
    pm, pp, po = rem(p + 3, 4), rem(p + 1, 4), rem(p + 2, 4)
    source = source or view
    a = net.send(source(po, 0), ra, minus)
    b = net.send(source(po, 1), rb, plus)
    c1 = net.send(source(pm, 1), rp.at[1], minus)
    c2 = net.send(source(pp, 0), rm.at[0], plus)
    yield
    a.wait_recv()

    def add_a():
        ra[...] = ra[...] + view(pm, 0)[...]

    def add_b():
        rb[...] = rb[...] + view(pp, 1)[...]
    net.work(0.1, add_a)
    d1 = net.send(ra, rp.at[0], minus)
    b.wait_recv()
    net.work(0.1, add_b)
    d2 = net.send(rb, rm.at[1], plus)
    yield
    for half, copies in ((0, (d1, c2)), (1, (c1, d2))):
        for copy in copies:
            copy.wait_recv()

        def total():
            put(half, view(p, half)[...].astype(F32) + rp[half].astype(F32) + rm[half].astype(F32))
        net.work(0.2, total)


def sum_yz(net, view, second_view, first, scratch, put, source=None):
    a1, b1, p1, m1, total, a2, b2, p2, m2 = scratch
    up_y, down_y, up_z, down_z = net.at(y=1), net.at(y=-1), net.at(z=1), net.at(z=-1)

    def keep(half, value):
        total[half] = value.astype(BF)
    source = source or view
    if first == "y":
        yield from sum_ring(net, lambda p, h: view(None, p, 2 + h, 1), net.y, up_y, down_y, a1, b1, p1, m1, keep,
                            lambda p, h: source(None, p, 2 + h, 1))
        yield from sum_ring(net, lambda p, h: second_view(total, p, None, h), net.z, up_z, down_z, a2, b2, p2, m2,
                            lambda h, v: put(2 + h, v))
    else:
        yield from sum_ring(net, lambda p, h: view(p, None, h, 1), net.z, up_z, down_z, a1, b1, p1, m1, keep,
                            lambda p, h: source(p, None, h, 1))
        yield from sum_ring(net, lambda p, h: second_view(total, None, p, h), net.y, up_y, down_y, a2, b2, p2, m2, put)


def columns_second(total, z, y, half):
    if y is not None:
        return total.at[half, :, y]
    return total.at[half, rem(z, 2), :, div(z, 2)]


def rows_second(total, z, y, half):
    if y is not None:
        return total.at[half, y]
    return total.at[half, rem(z, 2), div(z, 2)]


def sum_scratch(big, small):
    def vm(shape):
        return pltpu.VMEM(shape, BF)
    return [vm(big), vm(big), vm((2,) + big), vm((2,) + big), vm((2,) + big),
            vm(small), vm(small), vm((2,) + small), vm((2,) + small)]


def columns_scratch(n):
    return sum_scratch((2, 4, 16, n), (2, 16, n)) + sum_scratch((2, 2, 2, 16, n), (2, 16, n))


def rows_scratch(rows, n):
    return sum_scratch((4, rows, n // 4), (rows, n // 4)) + sum_scratch((2, 2, rows, n // 4), (rows, n // 4))


def exchange(net, src, dst):
    here = net.local(src.at[net.xc], dst.at[net.xc])
    copies = []
    for k in range(1, 8):
        to = rem(net.xc + k, 8)
        copies.append(net.send(src.at[to], dst.at[net.xc], net.peer(to)))
    yield
    here.wait()
    for copy in copies:
        copy.wait_recv()


def sum_columns(net, grad, scratch, reduced, dst, source=None, loaded=None):
    source = None if source is None else columns_view(source)
    def put(quarter, value):
        reduced[pl.ds(2 * quarter, 2)] = value.astype(BF)
    ways = [sum_yz(net, columns_view(grad), columns_second, "z", scratch[:9], put, source),
            sum_yz(net, columns_view(grad), columns_second, "y", scratch[9:], put, source)]
    for n in range(4):
        if n == 1 and loaded is not None:
            loaded()
        for way in ways:
            next(way)
        yield
    for way in ways:
        for _ in way:
            pass
    yield from exchange(net, reduced, dst)


def sum_rows(net, grad, scratch, dst):
    width = grad.shape[-1] // 4

    def put(quarter, value):
        dst[:, pl.ds(width * quarter, width)] = value
    ways = [sum_yz(net, rows_view(grad), rows_second, "z", scratch[:9], put),
            sum_yz(net, rows_view(grad), rows_second, "y", scratch[9:], put)]
    for _ in range(4):
        for way in ways:
            next(way)
        yield
    for way in ways:
        for _ in way:
            pass


def dot(a, b):
    return jnp.dot(a, b, preferred_element_type=F32)


def dot_right(a, b):
    return lax.dot_general(a, b, (((1,), (1,)), ((), ())), preferred_element_type=F32)


def dot_left(a, b):
    return lax.dot_general(a, b, (((0,), (0,)), ((), ())), preferred_element_type=F32)


def normalized(value):
    centred = value - jnp.mean(value, axis=1, keepdims=True)
    inv = lax.rsqrt(jnp.mean(centred * centred, axis=1, keepdims=True) + EPS)
    return centred * inv, inv


def normalize_back(grad, normed, inv, gain):
    scaled = grad * gain
    return inv * (scaled - jnp.mean(scaled, axis=1, keepdims=True)
                  - normed * jnp.mean(scaled * normed, axis=1, keepdims=True))


def chunk(t):
    return pl.ds(pl.multiple_of(t * 16, 16), 16)


def rotary_factors():
    angles = np.arange(LONGEST)[:, None] * THETA ** (-2.0 * np.arange(ROT // 2) / ROT)[None, :]
    cosine, sine = np.cos(angles), np.sin(angles)
    whole = np.zeros((128, 3, 2, 64), np.float32)
    whole[:LONGEST, 0] = 1.0
    for head in range(2):
        whole[:LONGEST, 0, head, :8] = cosine
        whole[:LONGEST, 0, head, 8:16] = cosine
        whole[:LONGEST, 1, head, :8] = -sine
        whole[:LONGEST, 2, head, 8:16] = sine
    whole = whole.reshape(128, 384)
    parts = []
    for _ in range(3):
        parts.append(whole.astype(BF))
        whole = whole - parts[-1].astype(np.float32)
    return np.stack(parts)


def factors(aux, table):
    both = dot(aux, table[0]) + dot(aux, table[1]) + dot(aux, table[2])
    return both[:, :128], both[:, 128:256], both[:, 256:]


def rotate(value, same, above, below):
    return value * same + pltpu.roll(value, 120, 1) * above + pltpu.roll(value, 8, 1) * below


def rotate_back(grad, same, above, below):
    return grad * same + pltpu.roll(grad * above, 8, 1) + pltpu.roll(grad * below, 120, 1)


def mask_of(aux):
    lane = lax.broadcasted_iota(jnp.int32, (128, 128), 1)
    row = lax.broadcasted_iota(jnp.int32, (128, 128), 0)
    marks = aux * jnp.where(lane >= 64, jnp.where(lane < 66, 1.0, 0.0), 0.0).astype(BF)
    same = dot_right(marks, marks)
    allowed = jnp.where(lane <= row, jnp.where(lane >= row - lax.rem(row, 64), same, 0.0), 0.0)
    bias = jnp.where(allowed > 0.5, 0.0, -1e30)
    return jnp.concatenate([bias, bias], axis=0)


def lanes_of_heads():
    lane = lax.broadcasted_iota(jnp.int32, (128, 128), 1)
    return (lane < 64).astype(F32)


def two_heads(value):
    first = lanes_of_heads()
    return jnp.concatenate([value * first.astype(BF), value * (1.0 - first).astype(BF)], axis=0)


def one_row(value):
    first = lanes_of_heads()
    return value[:128] * first + value[128:] * (1.0 - first)


def probabilities(queries, keys, bias):
    scores = dot_right(queries, keys) * 0.125 + bias
    shifted = jnp.exp(scores - jnp.max(scores, axis=1, keepdims=True))
    return shifted * (1.0 / jnp.sum(shifted, axis=1, keepdims=True))


def hidden_place(k, lanes):
    column = lax.broadcasted_iota(jnp.int32, (1, 384), 1)
    slot = lax.shift_right_logical(column * 1366, 16)
    unit = column - 48 * slot
    source = jnp.where(unit < 44, 352 * k % 128 + 44 * slot + unit, -1)
    row = lax.broadcasted_iota(jnp.int32, (lanes, 384), 0)
    return jnp.where(row == source, 1.0, 0.0).astype(BF)


def hidden_windows(k):
    width = 384 if 352 * k % 128 in (0, 32) else 512
    return [(zl, xc, (zl * 2816 + xc * 352) // 128 * 128) for zl in range(2) for xc in (k, k + 4)], width


def three_parts(value):
    parts = []
    for _ in range(3):
        parts.append(value.astype(BF).astype(F32))
        value = value - parts[-1]
    return parts


VMEM = pl.BlockSpec(memory_space=pltpu.VMEM)
ANY = pl.BlockSpec(memory_space=pl.ANY)


def sems(copies, locals_):
    return [pltpu.SemaphoreType.DMA((copies,)), pltpu.SemaphoreType.DMA((copies,)), pltpu.SemaphoreType.DMA((locals_,))]


def params(collective_id):
    return pltpu.CompilerParams(collective_id=collective_id, has_side_effects=True, vmem_limit_bytes=62 * 1024 * 1024)


def rings(net, *views):
    ways = [gather_yz(net, view, first) for view in views for first in ("y", "z")]
    for _ in range(4):
        for way in ways:
            next(way)
        yield
    for way in ways:
        for _ in way:
            pass


def spread_columns(net, pairs):
    zl, xc, zh, y = net.zl, net.xc, net.zh, net.y
    copies = [net.local(src(xc), dst.at[zl, xc, zh, y]) for src, dst in pairs]
    waits = []
    for src, dst in pairs:
        for k in range(1, 8):
            to = rem(xc + k, 8)
            waits.append(net.send(src(to), dst.at[zl, xc, zh, y], net.peer(to)))
    yield
    for copy in copies:
        copy.wait()
    for copy in waits:
        copy.wait_recv()
    yield from rings(net, *[columns_view(dst) for _, dst in pairs])


def spread_rows(net, src, dst):
    net.local(src, dst.at[net.zl, net.zh, net.y]).wait()
    yield from rings(net, rows_view(dst))


FRONT = ("MCVSMVMCMTCRMCSKRTCDRMSSAKCAERTVADRTABBAKVBEBADKBD", "VPAPEEPNBNAKBAANBKPAAANABABBBABBGBAGBOAHGBHAGOBGAG", "OA")


def front_kernel(tokens, cot, segments, qkv, gate, up, small, w_out_in, w_down_in, table,
                 vectors, sums, down_sum, h_keep, dh_keep, branch_all, qkv_keep, xn_keep, heads_keep,
                 mixed_keep, w_out_keep, aux_keep, out_part, grad_gate_keep, grad_up_keep, branch_own,
                 tokens_all, aux_all, aux_own, cot_all, w_qkv, small_all, w_out, w_down, w_gate, w_up, shared, heads, mixed,
                 xn, xn_all, hidden, dgate, dup, grad_down, grad_gate, h, dh, *rest):
    scratch = rest[0:5], rest[5:10]
    down_scratch, sem_refs = rest[10:28], rest[28:]
    net = Net(*sem_refs)
    x, c = net.x, net.c
    width, fw, count = 2048, 768, 512
    kept = {"tokens": net.local(tokens, xn)}

    def cut_qkv():
        for peer in range(8):
            for block in range(6):
                dgate[0, peer * 16:peer * 16 + 16, block * 128:block * 128 + 128] = (
                    qkv[:, block * 1024 + peer * 128:block * 1024 + peer * 128 + 128])

    def cut_down():
        last = jnp.concatenate([w_down_in[32:44].astype(F32), jnp.zeros((4, width), F32)], axis=0).astype(BF)
        w_down[net.zl, net.zh, net.y, 0:32] = w_down_in[0:32]
        w_down[net.zl, net.zh, net.y, 32:48] = last

    def cut_hidden():
        for k in range(4):
            windows, lanes = hidden_windows(k)
            place = hidden_place(k, lanes)
            rows = jnp.concatenate([ref[:, a:a + lanes] for ref in (gate, up) for _, _, a in windows], axis=0)
            value = dot(rows, place).astype(BF)
            for n in range(2):
                for m, (zlo, xc, _) in enumerate(windows):
                    at, row = (n * 4 + m) * 16, 128 + n * 128 + xc * 16
                    dgate[0, row:row + 16, zlo * 384:zlo * 384 + 384] = value[at:at + 16]

    def look():
        unit = (lax.broadcasted_iota(jnp.int32, (128, 128), 0)
                == lax.broadcasted_iota(jnp.int32, (128, 128), 1)).astype(F32).astype(BF)
        lane = lax.broadcasted_iota(jnp.int32, (64, 128), 1)
        for i in range(2):
            number = segments[i:i + 1]
            first = 64 - jnp.sum(number, axis=1, keepdims=True)
            slot = lax.broadcasted_iota(jnp.int32, (1, 64), 1)
            row = lax.broadcasted_iota(jnp.int32, (128, 64), 0)
            marks = jnp.where(row == slot - number * first, 1.0, 0.0) + jnp.where(row == number + 64, 1.0, 0.0)
            known = dot_left(marks.astype(BF), unit)
            value = xn[pl.ds(i * 64, 64)].astype(F32)
            mean = jnp.mean(value, axis=1, keepdims=True)
            centred = value - mean
            inv = lax.rsqrt(jnp.mean(centred * centred, axis=1, keepdims=True) + EPS)
            for n, part in enumerate(three_parts(mean) + three_parts(inv)):
                known = known + jnp.where(lane == 66 + n, part, 0.0)
            aux_own[i] = known.astype(BF)

    def clear():
        sums[...] = jnp.zeros_like(sums)
    net.work(0.1, cut_qkv)
    greet(net, True)

    def vectors_of():
        for block in range(16):
            total = jnp.sum(small_all[block // 8, block % 8].reshape(8, 16, 128).astype(F32), axis=0)
            vectors[:, block * 128:block * 128 + 128] = total

    def small_way():
        yield from spread_columns(net, [(lambda peer: small, small_all)])
        net.work(0.3, vectors_of)

    def columns_way():
        yield from spread_columns(net, [(lambda peer: dgate.at[0, pl.ds(pl.multiple_of(peer * 16, 16), 16)], w_qkv)])
        kept["qkv"] = net.local(w_qkv, qkv_keep)

    def hidden_way():
        net.work(2.0, cut_hidden)
        yield from spread_columns(net, [
            (lambda peer: dgate.at[0, pl.ds(pl.multiple_of(peer * 16 + 128, 16), 16)], w_gate),
            (lambda peer: dgate.at[0, pl.ds(pl.multiple_of(peer * 16 + 256, 16), 16)], w_up)])

    def down_weights_way():
        net.work(0.2, cut_down)
        yield from rings(net, rows_view(w_down))

    def tokens_way(i):
        if "tokens" in kept:
            kept.pop("tokens").wait()
            net.work(1.5, look)
            net.work(0.1, clear)
        rows = pl.ds(i * 64, 64)
        yield from gather_xc(net, (tokens.at[rows], tokens_all.at[i]), (aux_own.at[i], aux_all.at[i]))

    def out_way():
        yield from spread_rows(net, w_out_in, w_out)
        kept["out"] = net.local(w_out, w_out_keep)

    def half(i):
        net.need("ST"[i])
        net.need("M")

        def normalize_tokens():
            aux = aux_all[i].reshape(count, 128)
            row = lax.broadcasted_iota(jnp.int32, (128, 256), 0)
            lane = lax.broadcasted_iota(jnp.int32, (128, 256), 1)
            low = 66 + 3 * lax.div(lane, 128)
            pick = jnp.where(row >= low, jnp.where(row < low + 3, 1.0, 0.0), 0.0).astype(BF)
            both = dot(aux, pick)
            mean, inv = both[:, :128], both[:, 128:]

            @pl.loop(0, 16)
            def _(t):
                at = pl.ds(pl.multiple_of(t * 128, 128), 128)
                value = tokens_all[i, :, :, :, at].reshape(count, 128).astype(F32)
                value = (value - mean) * inv * vectors[0:1, at] + vectors[1:2, at]
                shared[i, :, :, :, at] = value.astype(BF).reshape(4, 2, 64, 128)
        net.work(2.0, normalize_tokens)
        kept["xn", i] = net.local(shared.at[i], xn_keep.at[i])
        kept["aux", i] = net.local(aux_all.at[i], aux_keep.at[i])
        yield
        net.need("C")

        def project():
            aux = aux_all[i].reshape(count, 128)
            same, above, below = factors(aux, table)
            xn_one = shared[i].reshape(count, width)
            for part in range(3):
                value = dot(xn_one, w_qkv[:, :, :, :, :, part * 256:part * 256 + 256].reshape(width, 256))
                for pair in range(2):
                    at = pl.ds(pair * 128, 128)
                    piece = value[:, pair * 128:pair * 128 + 128]
                    bias = jnp.sum(small_all[pair, net.xc].reshape(8, 16, 128).astype(F32), axis=0)[4 + part:5 + part]
                    piece = piece + bias
                    if part < 2:
                        piece = rotate(piece, same, above, below)
                    heads[i, part, :, at] = piece.astype(BF)
        net.work(4.0, project)
        kept["heads", i] = net.local(heads.at[i], heads_keep.at[i])
        yield

        def attend():
            @pl.loop(0, 4)
            def _(t):
                rows = pl.ds(pl.multiple_of(t * 128, 128), 128)
                bias = mask_of(aux_all[i, t].reshape(128, 128))
                for pair in range(2):
                    at = pl.ds(pair * 128, 128)
                    probs = probabilities(two_heads(heads[i, 0, rows, at]), heads[i, 1, rows, at], bias)
                    mixed[i, rows, at] = one_row(dot(probs.astype(BF), heads[i, 2, rows, at])).astype(BF)
        net.work(3.0, attend)
        kept["mixed", i] = net.local(mixed.at[i], mixed_keep.at[i])
        yield
        net.need("R")
        kept["xn", i].wait()

        def branch():
            @pl.loop(0, 4)
            def _(t):
                cols = pl.ds(pl.multiple_of(t * 512, 512), 512)
                value = dot(mixed[i], w_out[:, :, :, :, cols].reshape(256, 512))
                shared[i, :, :, :, cols] = value.astype(BF).reshape(4, 2, 64, 512)
        net.work(1.0, branch)

        def own(k):
            return shared.at[i, k, c]

        def theirs(k):
            return shared.at[i, k, 1 - c]
        yield from sum_xc(net, theirs, own, *scratch[i])
        net.drain("AB"[i])

        def normalize_branch():
            @pl.loop(0, 4, unroll=True)
            def _(t):
                rows, at = chunk(t), chunk(i * 4 + t)
                total = tokens_all[i, x, c, rows].astype(F32) + four_terms(net, own, scratch[i], rows)
                h[at] = total
                normed, _ = normalized(total)
                xn[at] = (normed * vectors[2:3] + vectors[3:4]).astype(BF)
        net.work(0.7, normalize_branch)
        kept["h", i] = net.local(h.at[pl.ds(i * 64, 64)], h_keep.at[pl.ds(i * 64, 64)])
        yield from gather_xc(net, (xn.at[pl.ds(i * 64, 64)], xn_all.at[i]))
        yield
        net.need("K" + "PN"[i])
        net.drain("CK")
        for j in range(fw // 256):
            def feed():
                at = pl.ds(j * 256, 256)
                inputs = xn_all[i].reshape(count, width)
                gate_val = dot(inputs, w_gate[:, :, :, :, :, at].reshape(width, 256))
                up_val = dot(inputs, w_up[:, :, :, :, :, at].reshape(width, 256))
                grad = dup[i, :, at].astype(F32)
                sigmoid = jax.nn.sigmoid(gate_val)
                active = gate_val * sigmoid
                hidden[i, :, at] = (active * up_val).astype(BF)
                dgate[i, :, at] = (grad * up_val * sigmoid * (1.0 + gate_val * (1.0 - sigmoid))).astype(BF)
                dup[i, :, at] = (grad * active).astype(BF)
            net.work(2.0, feed)
            yield
        net.mark("fed")
        net.drain("AB"[i])

        def back(zlo):
            @pl.loop(0, 4)
            def _(t):
                two = pl.ds(2 * t, 2)
                value = dot_right(dgate[i], w_gate[zlo, two].reshape(256, fw))
                value = value + dot_right(dup[i], w_up[zlo, two].reshape(256, fw))
                at = pl.ds(pl.multiple_of(zlo * 1024 + t * 256, 256), 256)
                shared[i, :, :, :, at] = value.astype(BF).reshape(4, 2, 64, 256)
        net.work(1.5, lambda: back(0))
        yield
        net.work(1.5, lambda: back(1))
        yield from sum_xc(net, theirs, own, *scratch[i])

        def normalize_again():
            @pl.loop(0, 4, unroll=True)
            def _(t):
                rows, at = chunk(t), chunk(i * 4 + t)
                grad = four_terms(net, own, scratch[i], rows)
                normed, inv = normalized(h[at])
                sums[0:1] += jnp.sum(grad * normed, axis=0, keepdims=True)
                sums[1:2] += jnp.sum(grad, axis=0, keepdims=True)
                total = cot_all[i, x, c, rows].astype(F32) + normalize_back(grad, normed, inv, vectors[2:3])
                dh[at] = total
                xn[at] = total.astype(BF)
        net.work(0.7, normalize_again)
        kept["dh", i] = net.local(dh.at[pl.ds(i * 64, 64)], dh_keep.at[pl.ds(i * 64, 64)])
        if i == 0:
            yield from gather_xc(net, (xn.at[pl.ds(0, 64)], branch_all))
        else:
            kept["branch"] = net.local(xn.at[pl.ds(64, 64)], branch_own)

    def w_down_rows(j):
        pieces, row = [], 256 * j
        while row < 256 * j + 256:
            slot, first = divmod(row, 48)
            size = min(48 - first, 256 * j + 256 - row)
            pieces.append(w_down[slot // 8, slot // 4 % 2, slot % 4, first:first + size])
            row += size
        return jnp.concatenate(pieces, axis=0)

    def down_way():
        net.need("AB", "fed")

        def compute(zlo):
            left = hidden[:, :, pl.ds(zlo * (fw // 2), fw // 2)].reshape(2 * count, fw // 2).T
            for t in range(width // 512):
                cols = pl.ds(t * 512, 512)
                value = dot(left, cot_all[:, :, :, :, cols].reshape(2 * count, 512))
                grad_down[zlo, :, :, :, cols] = value.astype(BF).reshape(2, 4, fw // 16, 512)
        net.work(1.8, lambda: compute(0))
        yield
        net.work(1.8, lambda: compute(1))
        yield from sum_rows(net, grad_down, down_scratch, down_sum)

    def gate_up_way():
        net.need("AB", "fed")
        kept["qkv"].wait()
        net.drain("C")

        def compute(zlo):
            @pl.loop(0, 4)
            def _(t):
                cols = pl.ds(pl.multiple_of(zlo * 1024 + t * 256, 256), 256)
                left = xn_all[:, :, :, :, cols].reshape(2 * count, 256).T
                for right, dst in ((dgate, grad_gate), (dup, w_qkv)):
                    value = dot(left, right[...].reshape(2 * count, fw))
                    dst[zlo, pl.ds(2 * t, 2)] = value.astype(BF).reshape(2, 2, 4, 16, fw)
        net.work(3.0, lambda: compute(0))
        yield
        net.work(3.0, lambda: compute(1))
        kept["gate"] = net.local(grad_gate, grad_gate_keep)
        kept["up"] = net.local(w_qkv, grad_up_keep)

    def result_way():
        for i in range(2):
            net.need("AB"[i], "fed")
            net.drain("ST"[i])

            def compute():
                @pl.loop(0, 8)
                def _(t):
                    cols = pl.ds(pl.multiple_of(t * 256, 256), 256)
                    value = dot(hidden[i], w_down[:, :, :, :, cols].reshape(fw, 256))
                    tokens_all[i, :, :, :, cols] = value.astype(BF).reshape(4, 2, 64, 256)
            net.work(1.5, compute)
            kept["part", i] = net.local(tokens_all.at[i], out_part.at[i])
            yield

    def hidden_back(i):
        net.need("V" + "DE"[i])
        for j in range(fw // 256):
            def compute():
                dup[i, :, pl.ds(j * 256, 256)] = dot_right(cot_all[i].reshape(count, width), w_down_rows(j)).astype(BF)
            net.work(0.9, compute)
            yield

    rows = [pl.ds(0, 64), pl.ds(64, 64)]
    play(net, FRONT, M=small_way(), C=columns_way(), R=out_way(), V=down_weights_way(), K=hidden_way(),
         S=tokens_way(0), T=tokens_way(1),
         D=gather_xc(net, (cot.at[rows[0]], cot_all.at[0])), E=gather_xc(net, (cot.at[rows[1]], cot_all.at[1])),
         A=half(0), B=half(1), G=down_way(), H=gate_up_way(), O=result_way(),
         P=hidden_back(0), N=hidden_back(1))
    for name in ("out", "gate", "up", "branch"):
        kept[name].wait()
    for name in ("h", "dh", "aux", "heads", "mixed", "part"):
        for i in range(2):
            kept[name, i].wait()
    net.finish()


BACK = ("NGACUDNAACDNANGBBBUCAQGQQBGACBUQOBAGDUQBSOUQSOQGSO", "USDOQ")


def back_kernel(tokens_in, h_in, dh_in, vectors, ln2_sums, table, branch_all, qkv_keep, xn_keep, heads_keep, mixed_keep,
                w_out_keep, aux_keep, out_part, grad_gate_keep, grad_up_keep, branch_own,
                grad_tokens, out, out_sum, small_out, gate_sum, up_sum, qkv_sum,
                branch, part_out, grad_gate, grad_up, w_qkv, w_out, xn_one, heads, mixed, aux, shared, dprojected, grad_qkv,
                grad_out, tokens, h, dh, sums, bias_sums, small_in, small_group, small_y, small_z, gate_reduced, up_reduced, qkv_reduced, *rest):
    scratch_in, scratch_out = (rest[0:5], rest[5:10]), (rest[10:15], rest[15:20])
    gate_scratch, up_scratch, qkv_scratch, out_scratch = rest[20:38], rest[38:56], rest[56:74], rest[74:92]
    sem_refs = rest[92:]
    net = Net(*sem_refs)
    x, c = net.x, net.c
    width, count, part_w = 2048, 512, 768
    sources = {"branch0": (branch_all, branch.at[0]), "w_out": (w_out_keep, w_out), "heads": (heads_keep, heads),
               "aux": (aux_keep, aux), "w_qkv": (qkv_keep, w_qkv), "gate": (grad_gate_keep, grad_gate),
               "out0": (out_part.at[0, :, c], part_out.at[0]), "out1": (out_part.at[1, :, c], part_out.at[1]),
               "up": (grad_up_keep, grad_up), "tokens": (tokens_in, tokens),
               "h": (h_in, h), "dh": (dh_in, dh), "mixed": (mixed_keep, mixed), "xn": (xn_keep, xn_one)}
    loads = {}

    def start(*names):
        for name in names:
            if name in sources:
                loads[name] = net.local(*sources.pop(name))

    def ready(*names):
        start(*names)
        for name in names:
            if name in loads:
                loads.pop(name).wait()
    start("branch0", "w_out", "heads", "aux", "gate")
    greet(net, True, True)

    def clear():
        sums[...] = jnp.zeros_like(sums)
        bias_sums[...] = jnp.zeros_like(bias_sums)
    net.work(0.1, clear)

    def half(i):
        if i == 0:
            ready("branch0")
        else:
            net.need("N")
        ready("w_out", "heads", "aux")
        start("out0", "gate", "out1", "w_qkv")

        def branch_back():
            value = dot_right(branch[i].reshape(count, width), w_out[...].reshape(256, width))
            dprojected[i, :, 512:] = value.astype(BF)
        net.work(0.8, branch_back)
        start("up", "mixed", "tokens", "dh", "h", "xn")
        yield

        def attend_back(tiles):
            @pl.loop(*tiles)
            def _(t):
                rows = pl.ds(pl.multiple_of(t * 128, 128), 128)
                marks = aux[i, t].reshape(128, 128)
                bias = mask_of(marks)
                same, above, below = factors(marks, table)
                for pair in range(2):
                    at = pl.ds(pair * 128, 128)
                    queries, keys = two_heads(heads[i, 0, rows, at]), heads[i, 1, rows, at]
                    probs = probabilities(queries, keys, bias)
                    grads = two_heads(dprojected[i, rows, pl.ds(512 + pair * 128, 128)])
                    dprobs = dot_right(grads, heads[i, 2, rows, at])
                    dscores = probs * (dprobs - jnp.sum(probs * dprobs, axis=1, keepdims=True))
                    dscores = dscores.astype(BF)
                    dvalues = dot_left(probs.astype(BF), grads)
                    dqueries = one_row(dot(dscores, keys)) * 0.125
                    dkeys = dot_left(dscores, queries) * 0.125
                    pieces = (rotate_back(dqueries, same, above, below), rotate_back(dkeys, same, above, below), dvalues)
                    for k, piece in enumerate(pieces):
                        low = piece.astype(BF)
                        dprojected[i, rows, pl.ds(k * 256 + pair * 128, 128)] = low
                        where = pl.ds(k * 256 + pair * 128, 128)
                        bias_sums[0:1, where] += jnp.sum(low.astype(F32), axis=0, keepdims=True)
        net.work(2.3, lambda: attend_back((0, 2)))
        yield
        net.work(2.3, lambda: attend_back((2, 4)))
        net.mark("attended")
        yield
        ready("w_qkv")

        def inputs_back():
            @pl.loop(0, 8)
            def _(t):
                weights = w_qkv[lax.div(t, 4), pl.ds(2 * lax.rem(t, 4), 2)].reshape(256, part_w)
                value = dot_right(dprojected[i], weights)
                shared[i, :, :, :, pl.ds(pl.multiple_of(t * 256, 256), 256)] = value.astype(BF).reshape(4, 2, 64, 256)
        net.work(1.5, inputs_back)

        def own(k):
            return shared.at[i, k, c]
        yield from sum_xc(net, lambda k: shared.at[i, k, 1 - c], own, *scratch_in[i])

        ready("tokens", "dh")

        def normalize_inputs():
            @pl.loop(0, 4, unroll=True)
            def _(t):
                rows, at = chunk(t), chunk(i * 4 + t)
                grad = four_terms(net, own, scratch_in[i], rows)
                normed, inv = normalized(tokens[at].astype(F32))
                sums[0:1] += jnp.sum(grad * normed, axis=0, keepdims=True)
                sums[1:2] += jnp.sum(grad, axis=0, keepdims=True)
                grad_tokens[at] = dh[at] + normalize_back(grad, normed, inv, vectors[0:1])
        net.work(0.7, normalize_inputs)

    def small_way():
        net.need("AB")

        def cut():
            sums[2:4] = ln2_sums[0:2]
            for k in range(8):
                for zl in range(2):
                    small_in[k, :, zl * 128:zl * 128 + 128] = sums[:, zl * 1024 + k * 128:zl * 1024 + k * 128 + 128]
        net.work(0.2, cut)
        yield from exchange(net, small_in, small_group)

        def add_group():
            total = small_group[0]
            for k in range(1, 8):
                total = total + small_group[k]
            small_y[0] = total
            for k in range(3):
                small_y[0, 4 + k:5 + k] = bias_sums[0:1, k * 256:k * 256 + 256]
        net.work(0.1, add_group)
        copies = [net.send(small_y.at[0], small_y.at[k], net.at(y=k)) for k in (1, 2, 3)]
        yield
        for copy in copies:
            copy.wait_recv()

        def add_y():
            small_z[0] = small_y[0] + small_y[1] + small_y[2] + small_y[3]
        net.work(0.1, add_y)
        copies = [net.send(small_z.at[0], small_z.at[k], net.at(z=k)) for k in (1, 2, 3)]
        yield
        for copy in copies:
            copy.wait_recv()

        def add_z():
            small_out[...] = small_z[0] + small_z[1] + small_z[2] + small_z[3]
        net.work(0.1, add_z)

    def result_way(i):
        ready("out%d" % i)

        def own(k):
            return part_out.at[i, k]
        yield from sum_xc(net, lambda k: out_part.at[i, k, 1 - c], own, *scratch_out[i])

        ready("h")

        def finish():
            @pl.loop(0, 4, unroll=True)
            def _(t):
                rows, at = chunk(t), chunk(i * 4 + t)
                out[at] = (h[at] + four_terms(net, own, scratch_out[i], rows)).astype(BF)
        net.work(0.5, finish)

    def columns_grad(left, right, dst):
        for zlo in range(2):
            def compute():
                @pl.loop(0, 4)
                def _(t):
                    cols = pl.ds(pl.multiple_of(zlo * 1024 + t * 256, 256), 256)
                    value = dot_left(left[:, :, :, :, cols].reshape(2 * count, 256), right[...].reshape(2 * count, part_w))
                    dst[zlo, pl.ds(2 * t, 2)] = value.astype(BF).reshape(2, 2, 4, 16, part_w)
            net.work(1.6, compute)
            yield

    def up_way():
        start("up")
        yield from sum_columns(net, grad_up, up_scratch, up_reduced, up_sum, grad_up_keep, lambda: ready("up"))

    def gate_way():
        start("gate")
        yield from sum_columns(net, grad_gate, gate_scratch, gate_reduced, gate_sum, grad_gate_keep, lambda: ready("gate"))

    def qkv_way():
        net.need("AB", "attended")
        ready("xn")
        yield from columns_grad(xn_one, dprojected, grad_qkv)
        yield from sum_columns(net, grad_qkv, qkv_scratch, qkv_reduced, qkv_sum)

    def out_way():
        ready("mixed", "branch0")
        net.need("N")

        def compute():
            left = mixed[...].reshape(2 * count, 256).T
            for t in range(4):
                cols = pl.ds(t * 512, 512)
                value = dot(left, branch[:, :, :, :, cols].reshape(2 * count, 512))
                grad_out[:, :, :, :, cols] = value.astype(BF).reshape(2, 2, 4, 16, 512)
        net.work(1.5, compute)
        yield from sum_rows(net, grad_out, out_scratch, out_sum)

    play(net, BACK, N=gather_xc(net, (branch_own, branch.at[1])), G=gate_way(), A=half(0), B=half(1), S=small_way(), C=result_way(0), D=result_way(1), Q=qkv_way(), U=up_way(), O=out_way())
    net.finish()


def finish_kernel(out_in, tokens_in, qkv_in, gate_in, up_in, down_in, w_out_in, small_in,
                  out, grad_tokens, grad_qkv, grad_out, grad_gate, grad_up, grad_down, ln1_gain, ln1_bias, ln2_gain, ln2_bias,
                  qkv_bias):
    out[...] = out_in[...]
    grad_tokens[...] = tokens_in[...]
    grad_out[...] = w_out_in[...]
    first = lax.div(lax.axis_index("fsdp"), 8) * 128 + lax.axis_index("dp") * 16
    mine = pltpu.roll(small_in[...], lax.rem(256 - first, 256), 1)[:, :16]
    for n, ref in enumerate((ln1_gain, ln1_bias, ln2_gain, ln2_bias)):
        ref[...] = mine[n:n + 1]
    qkv_bias[...] = mine[4:7]
    grad_down[...] = down_in[0:44]
    for peer in range(8):
        for block in range(6):
            grad_qkv[:, block * 1024 + peer * 128:block * 1024 + peer * 128 + 128] = (
                qkv_in[peer, :, block * 128:block * 128 + 128].astype(F32))
    grad_gate[...] = jnp.zeros_like(grad_gate)
    grad_up[...] = jnp.zeros_like(grad_up)
    for k in range(4):
        windows, lanes = hidden_windows(k)
        place = hidden_place(k, lanes)
        rows = jnp.concatenate(
            [ref[xc, :, zlo * 384:zlo * 384 + 384] for ref in (gate_in, up_in) for zlo, xc, _ in windows], axis=0)
        value = dot_right(rows, place)
        for n, ref in enumerate((grad_gate, grad_up)):
            for m, (_, _, a) in enumerate(windows):
                at = (n * 4 + m) * 16
                ref[:, a:a + lanes] += value[at:at + 16]


def shape(dims, kind):
    return jax.ShapeDtypeStruct(dims, kind)


def per_device(tokens, segment_ids, ln1_gain, ln1_bias, w_qkv, qkv_bias, w_out, ln2_gain, ln2_bias, w_gate, w_up, w_down,
               cotangent):
    rows, width = tokens.shape
    own_hidden = w_down.shape[0]
    padded = (own_hidden + 15) // 16 * 16
    part = 3 * width // 8
    fw = 16 * padded
    own_dp = lax.axis_index("dp")

    own = jnp.concatenate([jnp.stack([ln1_gain, ln1_bias, ln2_gain, ln2_bias], axis=0), qkv_bias], axis=0)
    lane = jnp.arange(128)[None, :]
    small = jnp.where(lane // 16 == own_dp, jnp.tile(jnp.pad(own, ((0, 9), (0, 0))), (1, 8)), jnp.zeros((), BF))
    table = rotary_factors()

    group = (2, 4, 2, rows // 2, width)
    columns = (2, 8, 2, 4, 16, fw)
    heads = (2, 3, 4 * rows, 256)

    def vm(dims, kind=BF):
        return pltpu.VMEM(dims, kind)

    front = pl.pallas_call(
        front_kernel,
        out_shape=(shape((16, width), F32), shape((8, width), F32), shape((padded, width), F32),
                   shape((rows, width), F32), shape((rows, width), F32), shape(group[1:], BF),
                   shape(columns, BF), shape(group, BF), shape(heads, BF), shape((2, 4 * rows, 256), BF),
                   shape((2, 2, 4, 16, width), BF), shape((2, 4, 2, rows // 2, 128), BF), shape(group, BF),
                   shape(columns, BF), shape(columns, BF), shape((rows // 2, width), BF)),
        in_specs=[ANY, ANY] + [VMEM] * 4 + [ANY, ANY] + [VMEM] * 2,
        out_specs=[VMEM] * 3 + [ANY] * 13,
        scratch_shapes=[
            vm(group), vm((2, 4, 2, rows // 2, 128)), vm((2, rows // 2, 128)), vm(group), vm(columns), vm((2, 8, 2, 4, 16, 128)), vm((2, 2, 4, 16, width)),
            vm((2, 2, 4, padded, width)), vm(columns), vm(columns), vm(group), vm(heads), vm((2, 4 * rows, 256)),
            vm((rows, width)), vm(group), vm((2, 4 * rows, fw)), vm((2, 4 * rows, fw)), vm((2, 4 * rows, fw)),
            vm((2, 2, 4, padded, width)), vm(columns), vm((rows, width), F32), vm((rows, width), F32)]
        + sum_xc_scratch(rows // 2, width) * 2 + rows_scratch(padded, width) + sems(300, 40),
        compiler_params=params(1), name="front",
    )(tokens, cotangent, segment_ids, w_qkv, w_gate, w_up, small, w_out, w_down, table)
    vectors, ln2_sums, down_sum, h, dh, branch_all, *keep = front

    grad_tokens, out, out_sum, small_sum, gate_sum, up_sum, qkv_sum = pl.pallas_call(
        back_kernel,
        out_shape=(shape((rows, width), F32), shape((rows, width), BF), shape((16, width), F32), shape((8, 256), F32),
                   shape((8, 16, fw), BF), shape((8, 16, fw), BF), shape((8, 16, part), BF)),
        in_specs=[ANY] * 3 + [VMEM] * 3 + [ANY] * 11,
        out_specs=[VMEM] * 4 + [ANY] * 3,
        scratch_shapes=[
            vm(group), vm((2, 4, rows // 2, width)), vm(columns), vm(columns), vm(columns), vm((2, 2, 4, 16, width)), vm(group),
            vm(heads), vm((2, 4 * rows, 256)), vm((2, 4, 2, rows // 2, 128)), vm(group), vm((2, 4 * rows, part)), vm(columns),
            vm((2, 2, 4, 16, width)), vm((rows, width)), vm((rows, width), F32), vm((rows, width), F32),
            vm((8, width), F32), vm((8, part), F32), vm((8, 8, 256), F32), vm((8, 8, 256), F32),
            vm((4, 8, 256), F32), vm((4, 8, 256), F32), vm((8, 16, fw)), vm((8, 16, fw)), vm((8, 16, part))]
        + sum_xc_scratch(rows // 2, width) * 4 + columns_scratch(fw) * 2 + columns_scratch(part) + rows_scratch(16, width)
        + sems(190, 24),
        compiler_params=params(2), name="back",
    )(tokens, h, dh, vectors, ln2_sums, table, branch_all, *keep)

    vector = shape((1, 16), F32)
    out, grad_tokens, grad_w_qkv, grad_w_out, grad_w_gate, grad_w_up, grad_w_down, *vectors, grad_bias = pl.pallas_call(
        finish_kernel,
        out_shape=(shape((rows, width), BF), shape((rows, width), F32), shape((16, 3 * width), F32), shape((16, width), F32),
                   shape((16, 128 * own_hidden), F32), shape((16, 128 * own_hidden), F32), shape((own_hidden, width), F32),
                   vector, vector, vector, vector, shape((3, 16), F32)),
        in_specs=[VMEM] * 8, out_specs=[VMEM] * 12, scratch_shapes=[],
        compiler_params=pltpu.CompilerParams(vmem_limit_bytes=61 * 1024 * 1024), name="finish",
    )(out, grad_tokens, qkv_sum, gate_sum, up_sum, down_sum, out_sum, small_sum)
    vectors = [value.reshape(16) for value in vectors]
    return (out, grad_tokens, vectors[0], vectors[1], grad_w_qkv, grad_bias, grad_w_out, vectors[2], vectors[3], grad_w_gate,
            grad_w_up, grad_w_down)


def solution(mesh):
    spread = P(("fsdp", "dp"), None)
    vector = P(("fsdp", "dp"))
    bias = P(None, ("fsdp", "dp"))
    return jax.shard_map(
        per_device,
        mesh=mesh,
        in_specs=(spread, spread, vector, vector, spread, bias, spread, vector, vector, spread, spread, spread, spread),
        out_specs=(spread, spread, vector, vector, spread, bias, spread, vector, vector, spread, spread, spread),
        check_vma=False,
    )
```
